32 devices in a mesh: groups: 1, tensor: 16 (over z, y, x), sub: 2 (over core).
Axes of the slice: x: 2, y: 2, z: 4, core: 2. Of those that a mesh axis runs over, the one named last changes fastest.
Arguments:
- stored: bfloat16 [8192, 32768], P(('tensor', 'sub')), may hold values from -0.0625 to 0.0625
- tokens: bfloat16 [256, 8192], P(('groups', 'tensor')), may hold values from -6 to 6
- owner_map: int32 [256], replicated, may hold values from 0 to 255, each once
- live_count: int32 [1], P('groups'), may hold values from 128 to 256
Outputs:
- serving_out: bfloat16 [256, 32768], P('groups', ('tensor', 'sub'))
The draws below stay inside these ranges and needn't reach their ends.
Inputs may be any that keep to these rules, and one draw needn't show every extreme that they name: `owner_map`: each of the 256 saved column blocks is named exactly once. Rows from live_count on are padding.
All inputs are finite; a program needn't handle non-finite values.
Results may differ from the reference program's by a relative error of at most 0.001.
Values may be sent and summed in bfloat16 or wider, within the bound.
No kernel may reach another device: no remote copies, remote signals or barrier semaphores. Data moves between devices by JAX's collectives and lax.ppermute only.
A program may use at most 128 MiB of HBM per device.

```python
import jax
import jax.numpy as jnp

D = 8192
FF = 32768
BLOCK = 128
TOKENS = 256
NB = 256


def block_levels(rng, extent, cuts, least, top_value):
    factor_of = 1.0
    for axis_at, shards_of in cuts:
        heights = jax.random.uniform(jax.random.fold_in(jax.random.fold_in(rng, 6), axis_at), (shards_of,), jnp.float32, least / len(cuts), top_value / len(cuts))
        factor_of = factor_of * jnp.repeat(jnp.exp(heights), extent[axis_at] // shards_of).reshape((-1,) + (1,) * (len(extent) - 1 - axis_at))
    return factor_of


def noise(key, dims, width, most, cuts=(), kind=jnp.bfloat16):
    factor_of = block_levels(key, dims, cuts, -0.22, 0.18) if cuts else 1.0
    array = jax.random.normal(key, dims, jnp.float32) * width * factor_of
    return jnp.minimum(jnp.maximum(array, -most), most).astype(kind)


def setup_inputs(seed: int = 0, part: int = 0) -> dict:
    seeds = jax.random.split(jax.random.key(seed), 5)
    part_keys = jax.random.split(jax.random.fold_in(seeds[4], part), 5)
    stored = noise(seeds[0], (D, FF), D ** -0.5, 0.0625, ((0, 32),))
    tokens = noise(part_keys[1], (TOKENS, D), 1.0, 6.0, ((0, 16),))
    owner_map = jax.random.permutation(seeds[2], NB).astype(jnp.int32)
    live_count = jax.random.randint(part_keys[3], (1,), TOKENS // 2, TOKENS + 1).astype(jnp.int32)
    return {"stored": stored, "tokens": tokens, "owner_map": owner_map, "live_count": live_count}


def reference(stored, tokens, owner_map, live_count):
    product = jnp.dot(tokens, stored, preferred_element_type=jnp.float32)
    regrouped = jnp.take(product.reshape(TOKENS, NB, BLOCK), owner_map, axis=1).reshape(TOKENS, FF)
    row_ids = jnp.arange(TOKENS, dtype=jnp.int32)
    keep = (row_ids < live_count[0])[:, None]
    return jnp.where(keep, regrouped, jnp.float32(0.0)).astype(jnp.bfloat16)
```

```python
import functools

import jax
import jax.numpy as jnp
from jax import lax
from jax.experimental import pallas as pl
from jax.experimental.pallas import tpu as pltpu
from jax.sharding import PartitionSpec as P

STEPS = 128.0
TOP = 32000.0
TILE = 16
VMEM = 40 * 1024 * 1024


def flow_orders(bits):
    straight = list(range(bits))
    orders = [straight, straight[1:] + straight[:1], straight[2:3] + straight[:2] + straight[3:]]
    return orders[: max(1, min(3, bits))]


def flow_blocks(per_dev, flows):
    flows = min(flows, per_dev)
    counts = [per_dev // flows + (1 if f < per_dev % flows else 0) for f in range(flows)]
    firsts = [sum(counts[:f]) for f in range(flows)]
    return list(zip(firsts, counts))


class Flow:
    def __init__(self, order, first, count, per_dev, width, chips):
        self.order, self.first, self.count = order, first, count
        self.per_dev, self.width, self.chips = per_dev, width, chips
        self.bits = len(order)
        self.cols = count * width

    def block_id(self, owner, meta, place, j, sub):
        flipped = 0
        for s, bit in enumerate(self.order):
            flipped = flipped + (((place >> (self.bits - 1 - s)) & 1) << bit)
        dest = meta[0] ^ flipped
        return owner[(dest * 2 + sub) * self.per_dev + self.first + j]

    def send_range(self, stage):
        return self.chips >> (stage + 1)


def gather_kernel(n, owner, meta, *refs):
    out = refs[n]
    width = refs[0].shape[1]
    for k in range(n):
        out[:, k * width:(k + 1) * width] = refs[k][...]


def gather_for_sibling(stored, owner, meta, flow, low, count):
    rows = stored.shape[0]
    group = min(count, 4)
    n = group * flow.count

    def pick(k, i, owner, meta):
        return 0, flow.block_id(owner, meta, low + i * group + k // flow.count, k % flow.count, 1 - meta[1])

    return pl.pallas_call(
        functools.partial(gather_kernel, n),
        grid_spec=pltpu.PrefetchScalarGridSpec(
            num_scalar_prefetch=2,
            grid=(count // group,),
            in_specs=[pl.BlockSpec((rows, flow.width), functools.partial(pick, k)) for k in range(n)],
            out_specs=pl.BlockSpec((rows, n * flow.width), lambda i, owner, meta: (0, i)),
        ),
        out_shape=jax.ShapeDtypeStruct((rows, count * flow.cols), stored.dtype),
        compiler_params=pltpu.CompilerParams(vmem_limit_bytes=VMEM),
        cost_estimate=pl.CostEstimate(flops=0, bytes_accessed=4 * rows * count * flow.cols, transcendentals=0),
    )(owner, meta, *[stored] * n)


def decode_scale(code):
    return jnp.exp2(code * (1.0 / STEPS)) * (1.0 / TOP)


def partial_sum(n, prev, tok_own, tok_sib, refs):
    own = jnp.concatenate([refs[k][...] for k in range(n)], axis=1)
    total = jnp.dot(tok_own[...], own, preferred_element_type=jnp.float32)
    total = total + jnp.dot(tok_sib[...], refs[n][...], preferred_element_type=jnp.float32)
    main = total.shape[0] - TILE
    body, tail = total[:main], total[main:]
    for ref in refs[n + 1:n + 1 + prev]:
        last = ref[main:, :].astype(jnp.float32)
        scale = decode_scale(last[TILE - 1:, :])
        body = body + ref[:main, :].astype(jnp.float32) * scale
        tail = tail + last * scale
    return body, tail


def send_kernel(n, prev, owner, meta, tok_own, tok_sib, *refs):
    out = refs[n + 1 + prev]
    body, tail = partial_sum(n, prev, tok_own, tok_sib, refs)
    main = body.shape[0]
    is_code = lax.broadcasted_iota(jnp.int32, tail.shape, 0) == TILE - 1
    tail = jnp.where(is_code, 0.0, tail)
    top = jnp.maximum(jnp.max(jnp.abs(body), axis=0, keepdims=True), jnp.max(jnp.abs(tail), axis=0, keepdims=True))
    code = jnp.ceil(jnp.log2(jnp.maximum(top, 1e-30)) * STEPS)
    up = 1.0 / decode_scale(code)
    out[:main, :] = jnp.round(body * up).astype(jnp.int32).astype(jnp.int16)
    out[main:, :] = jnp.where(is_code, code, jnp.round(tail * up)).astype(jnp.int32).astype(jnp.int16)


def send_part(stored, owner, meta, tokens, sibling, arrived, flow, stage, low):
    rows = stored.shape[0]
    places = flow.send_range(stage)
    group = min(places, 2)
    n = group * flow.count
    cols = group * flow.cols
    height = tokens.shape[0]

    def pick(k, i, owner, meta):
        return 0, flow.block_id(owner, meta, places + i * group + k // flow.count, k % flow.count, meta[1])

    at = lambda first: (lambda i, owner, meta: (0, first // group + i))
    return pl.pallas_call(
        functools.partial(send_kernel, n, len(arrived)),
        grid_spec=pltpu.PrefetchScalarGridSpec(
            num_scalar_prefetch=2,
            grid=(places // group,),
            in_specs=[
                pl.BlockSpec((height, rows), lambda i, owner, meta: (0, meta[1])),
                pl.BlockSpec((height, rows), lambda i, owner, meta: (0, 1 - meta[1])),
                *[pl.BlockSpec((rows, flow.width), functools.partial(pick, k)) for k in range(n)],
                pl.BlockSpec((rows, cols), at(places - low)),
                *[pl.BlockSpec((height, cols), at(places)) for _ in arrived],
            ],
            out_specs=pl.BlockSpec((height, cols), at(0)),
        ),
        out_shape=jax.ShapeDtypeStruct((height, places * flow.cols), jnp.int16),
        compiler_params=pltpu.CompilerParams(vmem_limit_bytes=VMEM),
        cost_estimate=pl.CostEstimate(
            flops=4 * height * rows * places * flow.cols,
            bytes_accessed=(4 * rows + 2 * height * (1 + len(arrived))) * places * flow.cols,
            transcendentals=0,
        ),
    )(owner, meta, tokens, tokens, *[stored] * n, sibling, *arrived)


def last_kernel(flows, owner, meta, tok_own, tok_sib, *refs):
    out = refs[-1]
    live = meta[2]
    at = 0
    for flow in flows:
        body, tail = partial_sum(flow.count, flow.bits, tok_own, tok_sib, refs[at:])
        at += flow.count + 1 + flow.bits
        cols = slice(flow.first * flow.width, flow.first * flow.width + flow.cols)
        for first, part in ((0, body), (body.shape[0], tail)):
            size = min(part.shape[0], out.shape[0] - first)
            if size > 0:
                ids = first + lax.broadcasted_iota(jnp.int32, (size, part.shape[1]), 0)
                out[first:first + size, cols] = jnp.where(ids < live, part[:size], 0.0).astype(out.dtype)
        done = body.shape[0] + tail.shape[0]
        if done < out.shape[0]:
            out[done:, cols] = jnp.zeros((out.shape[0] - done, flow.cols), out.dtype)


def last_part(stored, owner, meta, tokens, siblings, arrived, flows, count):
    rows, height = stored.shape[0], tokens.shape[0]
    specs = [
        pl.BlockSpec((height, rows), lambda i, owner, meta: (0, meta[1])),
        pl.BlockSpec((height, rows), lambda i, owner, meta: (0, 1 - meta[1])),
    ]
    operands = [tokens, tokens]
    for flow, sibling, got in zip(flows, siblings, arrived):
        for j in range(flow.count):
            specs.append(pl.BlockSpec(
                (rows, flow.width),
                functools.partial(lambda f, j, i, owner, meta: (0, f.block_id(owner, meta, 0, j, meta[1])), flow, j)))
            operands.append(stored)
        specs.append(pl.BlockSpec((rows, flow.cols), lambda i, owner, meta: (0, 0)))
        operands.append(sibling)
        for part in got:
            specs.append(pl.BlockSpec((height, flow.cols), lambda i, owner, meta: (0, 0)))
            operands.append(part)
    cols = sum(flow.cols for flow in flows)
    return pl.pallas_call(
        functools.partial(last_kernel, flows),
        grid_spec=pltpu.PrefetchScalarGridSpec(
            num_scalar_prefetch=2,
            grid=(1,),
            in_specs=specs,
            out_specs=pl.BlockSpec((count, cols), lambda i, owner, meta: (0, 0)),
        ),
        out_shape=jax.ShapeDtypeStruct((count, cols), jnp.bfloat16),
        compiler_params=pltpu.CompilerParams(vmem_limit_bytes=VMEM),
    )(owner, meta, *operands)


def on_device(stored, tokens, owner_map, live_count):
    rows = stored.shape[0]
    block_count = owner_map.shape[0]
    width = stored.shape[1] // block_count
    chips = lax.axis_size("tensor")
    per_dev = block_count // (2 * chips)
    count = tokens.shape[0] * chips
    bits = chips.bit_length() - 1
    orders = flow_orders(bits)
    flows = [
        Flow(order, first, blocks, per_dev, width, chips)
        for order, (first, blocks) in zip(orders, flow_blocks(per_dev, len(orders)))
    ]
    meta = jnp.stack([lax.axis_index("tensor"), lax.axis_index("sub"), live_count[0]]).astype(jnp.int32)

    half = chips // 2
    swap = [(0, 1), (1, 0)]
    far = [lax.ppermute(gather_for_sibling(stored, owner_map, meta, f, half, half), "sub", swap) for f in flows]
    near = [lax.ppermute(gather_for_sibling(stored, owner_map, meta, f, 0, half), "sub", swap) for f in flows]

    part = lax.all_to_all(tokens, "tensor", split_axis=1, concat_axis=0, tiled=True)
    ids = lax.broadcasted_iota(jnp.int32, (count, 1), 0)
    part = jnp.where(ids < live_count[0], part, jnp.zeros((), part.dtype))
    height = count + TILE
    part = jnp.pad(part, ((0, height - count), (0, 0)))

    arrived = [[] for _ in flows]
    for stage in range(bits):
        for f, flow in enumerate(flows):
            low = half if stage == 0 else 0
            sent = send_part(stored, owner_map, meta, part, (far if stage == 0 else near)[f], arrived[f], flow, stage, low)
            step = 1 << flow.order[stage]
            arrived[f].append(lax.ppermute(sent, "tensor", [(c, c ^ step) for c in range(chips)]))
    return last_part(stored, owner_map, meta, part, near, arrived, flows, count)


def solution(mesh):
    placed = (P(("tensor", "sub"), None), P(("groups", "tensor"), None), P(), P("groups"))
    return jax.shard_map(
        on_device,
        mesh=mesh,
        in_specs=placed,
        out_specs=P("groups", ("tensor", "sub")),
        check_vma=False,
    )
```

```python
import functools

import jax
import jax.numpy as jnp
from jax import lax
from jax.experimental import pallas as pl
from jax.experimental.pallas import tpu as pltpu
from jax.sharding import PartitionSpec as P

STEPS = 128.0
TOP = 32000.0
LANES = 128
TILE = 16
VG = 48 * 1024 * 1024
VM = 16 * 1024 * 1024
VP = 16 * 1024 * 1024
VS = 16 * 1024 * 1024
VL = 16 * 1024 * 1024
GROUP = 2
WAIT = 96 * 1024 * 1024


def flow_orders(bits):
    straight = list(range(bits))
    orders = [straight, straight[1:] + straight[:1], straight[2:3] + straight[:2] + straight[3:]]
    return orders[: max(1, min(3, bits))]


def flow_blocks(per_dev, flows):
    flows = min(flows, per_dev)
    counts = [per_dev // flows + (1 if f < per_dev % flows else 0) for f in range(flows)]
    firsts = [sum(counts[:f]) for f in range(flows)]
    return list(zip(firsts, counts))


class Flow:
    def __init__(self, order, first, count, per_dev, width, chips):
        self.order, self.first, self.count = order, first, count
        self.per_dev, self.width, self.chips = per_dev, width, chips
        self.bits = len(order)
        self.cols = count * width

    def destination(self, place):
        return sum(((place >> (self.bits - 1 - s)) & 1) << bit for s, bit in enumerate(self.order))

    def spot(self, low):
        return self.first * self.chips + low * self.count


def block_lists(owner, flows):
    chip, sub = lax.axis_index("tensor"), lax.axis_index("sub")
    change = [flow.destination(p) for flow in flows for p in range(flow.chips) for _ in range(flow.count)]
    block = [flow.first + j for flow in flows for _ in range(flow.chips) for j in range(flow.count)]
    per_dev = flows[0].per_dev
    places = [((chip ^ jnp.array(change, jnp.int32)) * 2 + core) * per_dev + jnp.array(block, jnp.int32)
              for core in (sub, 1 - sub)]
    wanted = jnp.concatenate(places)[:, None]
    have = lax.broadcasted_iota(jnp.int32, (1, owner.shape[0]), 1)
    return jnp.sum(jnp.where(wanted == have, owner[None, :], 0), axis=1)


def lanes(index, width):
    return pl.ds(pl.multiple_of(index * width, width), width)


def gather_kernel(runs, width, ids, stored, out, held, sems, out_sems):
    def copy(at, block):
        return pltpu.make_async_copy(stored.at[:, lanes(block, width)], held.at[:, lanes(at, width)], sems.at[at])

    at = 0
    for first, size in runs:
        pl.loop(0, size)(lambda i, at=at, first=first: copy(at + i, ids[first + i]).start())
        at += size
    parts = out_sems.shape[0]
    size = at // parts

    def out_copy(j):
        cols = lanes(j, size * width)
        return pltpu.make_async_copy(held.at[:, cols], out.at[:, cols], out_sems.at[j])

    @pl.loop(0, parts)
    def _(j):
        pl.loop(0, size)(lambda i: copy(j * size + i, 0).wait())
        out_copy(j).start()

    pl.loop(0, parts)(lambda j: out_copy(j).wait())


def gather_for_sibling(stored, ids, flows, low, count):
    rows = stored.shape[0]
    width = flows[0].width
    runs = [(ids.shape[0] // 2 + flow.spot(low), count * flow.count) for flow in flows]
    blocks = sum(size for _, size in runs)
    return pl.pallas_call(
        functools.partial(gather_kernel, runs, width),
        in_specs=[pl.BlockSpec(memory_space=pltpu.SMEM), pl.BlockSpec(memory_space=pltpu.HBM)],
        out_specs=pl.BlockSpec(memory_space=pltpu.HBM),
        out_shape=jax.ShapeDtypeStruct((rows, blocks * width), stored.dtype),
        scratch_shapes=[
            pltpu.VMEM((rows, blocks * width), stored.dtype),
            pltpu.SemaphoreType.DMA((blocks,)),
            pltpu.SemaphoreType.DMA((count,)),
        ],
        compiler_params=pltpu.CompilerParams(vmem_limit_bytes=VG),
        cost_estimate=pl.CostEstimate(flops=0, bytes_accessed=rows, transcendentals=0),
    )(ids, stored)


def decode_scale(code):
    return jnp.exp2(code * (1.0 / STEPS)) * (1.0 / TOP)


def mask_kernel(meta, tok, out):
    rows = tok.shape[1] // 2
    size = min(out.shape[0], tok.shape[0])
    ids = lax.broadcasted_iota(jnp.int32, (size, rows), 0)
    for side in range(2):
        part = tok[:size, lanes(meta[1] ^ side, rows)]
        out[:size, side * rows:(side + 1) * rows] = jnp.where(ids < meta[2], part, jnp.zeros((), tok.dtype))
    if size < out.shape[0]:
        out[size:] = jnp.zeros((out.shape[0] - size, out.shape[1]), out.dtype)


def mask_tokens(height, meta, tokens):
    shape = (height, tokens.shape[1])
    return pl.pallas_call(
        mask_kernel,
        in_specs=[pl.BlockSpec(memory_space=pltpu.SMEM), pl.BlockSpec(memory_space=pltpu.VMEM)],
        out_specs=pl.BlockSpec(memory_space=pltpu.VMEM),
        out_shape=jax.ShapeDtypeStruct(shape, tokens.dtype),
        compiler_params=pltpu.CompilerParams(vmem_limit_bytes=VM),
        cost_estimate=pl.CostEstimate(flops=0, bytes_accessed=WAIT, transcendentals=0),
    )(meta, tokens)


def encode_loop(running, out):
    height = out.shape[0]
    main = height - TILE

    @pl.loop(0, out.shape[1] // LANES)
    def _(c):
        cols = lanes(c, LANES)
        total = running(cols)
        body, tail = total[:main], total[main:]
        is_code = lax.broadcasted_iota(jnp.int32, tail.shape, 0) == TILE - 1
        tail = jnp.where(is_code, 0.0, tail)
        top = jnp.max(jnp.abs(jnp.concatenate([body, tail], axis=0)), axis=0, keepdims=True)
        code = jnp.ceil(jnp.log2(jnp.maximum(top, 1e-30)) * STEPS)
        up = 1.0 / decode_scale(code)
        out[:main, cols] = jnp.round(body * up).astype(jnp.int32).astype(jnp.int16)
        out[main:, cols] = jnp.where(is_code, code, jnp.round(tail * up)).astype(jnp.int32).astype(jnp.int16)


def add_arrived(total, arrived, cols):
    height = total.shape[0]
    for part in arrived:
        code = part[height - TILE:, cols].astype(jnp.float32)[TILE - 1:, :]
        total = total + part[:, cols].astype(jnp.float32) * decode_scale(code)
    return total


def product_kernel(n, coded, ids, tok, *refs):
    out = refs[n + 1]
    own = jnp.concatenate([refs[k][...] for k in range(n)], axis=1)
    weights = jnp.concatenate([own, refs[n][...]], axis=0)
    total = jnp.dot(tok[...], weights, preferred_element_type=jnp.float32)
    if coded:
        held = refs[n + 2]
        held[...] = total
        encode_loop(lambda cols: held[:, cols], out)
    else:
        out[...] = total


def products(stored, ids, tokens, sibling, flow, low, count, sib_first, coded):
    rows = stored.shape[0]
    height = tokens.shape[0]
    group = min(count, GROUP)
    n = group * flow.count
    cols = group * flow.cols

    def pick(k, i, ids):
        return 0, ids[flow.spot(low) + i * n + k]

    kind = jnp.int16 if coded else jnp.float32
    return pl.pallas_call(
        functools.partial(product_kernel, n, coded),
        grid_spec=pltpu.PrefetchScalarGridSpec(
            num_scalar_prefetch=1,
            grid=(count // group,),
            in_specs=[
                pl.BlockSpec(tokens.shape, lambda i, ids: (0, 0)),
                *[pl.BlockSpec((rows, flow.width), functools.partial(pick, k)) for k in range(n)],
                pl.BlockSpec((rows, cols), lambda i, ids: (0, sib_first * flow.width // cols + i)),
            ],
            out_specs=pl.BlockSpec((height, cols), lambda i, ids: (0, i)),
            scratch_shapes=[pltpu.VMEM((height, cols), jnp.float32)] if coded else [],
        ),
        out_shape=jax.ShapeDtypeStruct((height, count * flow.cols), kind),
        compiler_params=pltpu.CompilerParams(vmem_limit_bytes=VP),
        cost_estimate=pl.CostEstimate(
            flops=4 * height * rows * count * flow.cols,
            bytes_accessed=(4 * rows + 4 * height) * count * flow.cols,
            transcendentals=0,
        ),
    )(ids, tokens, *[stored] * n, sibling)


def send_kernel(total, *refs):
    encode_loop(lambda cols: add_arrived(total[:, cols], refs[:-1], cols), refs[-1])


def send_part(total, arrived, flow, places):
    height = total.shape[0]
    group = max(1, places // 2)
    steps = places // group
    block = pl.BlockSpec((height, group * flow.cols), lambda i: (0, steps + i))
    return pl.pallas_call(
        send_kernel,
        grid=(steps,),
        in_specs=[block] * (1 + len(arrived)),
        out_specs=pl.BlockSpec((height, group * flow.cols), lambda i: (0, i)),
        out_shape=jax.ShapeDtypeStruct((height, places * flow.cols), jnp.int16),
        compiler_params=pltpu.CompilerParams(vmem_limit_bytes=VS),
        cost_estimate=pl.CostEstimate(
            flops=4 * height * places * flow.cols,
            bytes_accessed=(6 + 2 * len(arrived)) * height * places * flow.cols,
            transcendentals=0,
        ),
    )(total, *arrived)


def last_kernel(flows, meta, *refs):
    out = refs[-1]
    each = 1 + flows[0].bits
    height = refs[0].shape[0]
    size = min(height, out.shape[0])
    scales = [
        [decode_scale(part[height - TILE:, :].astype(jnp.float32)[TILE - 1:, :])
         for part in refs[f * each + 1:(f + 1) * each]]
        for f in range(len(flows))
    ]

    @pl.loop(0, size // TILE)
    def _(r):
        at = pl.ds(pl.multiple_of(r * TILE, TILE), TILE)
        for f, flow in enumerate(flows):
            x = refs[f * each][at, :]
            for part, scale in zip(refs[f * each + 1:(f + 1) * each], scales[f]):
                x = x + part[at, :].astype(jnp.float32) * scale
            ids = r * TILE + lax.broadcasted_iota(jnp.int32, x.shape, 0)
            cols = pl.ds(flow.first * flow.width, flow.cols)
            out[at, cols] = jnp.where(ids < meta[2], x, 0.0).astype(out.dtype)

    if size < out.shape[0]:
        out[size:] = jnp.zeros((out.shape[0] - size, out.shape[1]), out.dtype)


def last_part(count, meta, totals, arrived, flows):
    height = totals[0].shape[0]
    specs, operands = [], []
    for flow, total, got in zip(flows, totals, arrived):
        specs += [pl.BlockSpec((height, flow.cols), lambda i, meta: (0, 0))] * (1 + len(got))
        operands += [total, *got]
    cols = sum(flow.cols for flow in flows)
    return pl.pallas_call(
        functools.partial(last_kernel, flows),
        grid_spec=pltpu.PrefetchScalarGridSpec(
            num_scalar_prefetch=1,
            grid=(1,),
            in_specs=specs,
            out_specs=pl.BlockSpec((count, cols), lambda i, meta: (0, 0)),
        ),
        out_shape=jax.ShapeDtypeStruct((count, cols), jnp.bfloat16),
        compiler_params=pltpu.CompilerParams(vmem_limit_bytes=VL),
    )(meta, *operands)


def run(height, stored, tokens, owner_map, meta):
    block_count = owner_map.shape[0]
    width = stored.shape[1] // block_count
    chips = lax.axis_size("tensor")
    per_dev = block_count // (2 * chips)
    count = tokens.shape[0] * chips
    bits = chips.bit_length() - 1
    orders = flow_orders(bits)
    flows = [
        Flow(order, first, blocks, per_dev, width, chips)
        for order, (first, blocks) in zip(orders, flow_blocks(per_dev, len(orders)))
    ]

    part = lax.all_to_all(tokens, "tensor", split_axis=1, concat_axis=0, tiled=True)
    half = chips // 2
    ids = block_lists(owner_map, flows)
    swap = lambda x: lax.ppermute(x, "sub", [(0, 1), (1, 0)])
    gather = functools.partial(gather_for_sibling, stored)
    lead = min(1, len(flows) - 1)
    others = [f for f in range(len(flows)) if f != lead]
    first, later = lax.optimization_barrier((swap(gather(ids, [flows[lead]], half, half)), ids))
    far = {lead: (first, 0)}
    if others:
        rest = gather(later, [flows[f] for f in others], half, half)
        rest, later = lax.optimization_barrier((rest, later))
        rest = swap(rest)
        at = 0
        for f in others:
            far[f] = (rest, at)
            at += half * flows[f].count
    picked, part = lax.optimization_barrier((gather(later, flows, 0, half), part))
    near = swap(picked)
    part = mask_tokens(height, meta, part)

    def cross(x, bit):
        return lax.ppermute(x, "tensor", [(c, c ^ (1 << bit)) for c in range(chips)])

    arrived, totals = [], []
    for f, flow in enumerate(flows):
        sibling, at = far[f]
        sent = products(stored, ids, part, sibling, flow, half, half, at, True)
        arrived.append([cross(sent, flow.order[0])])
    for flow in flows:
        totals.append(products(stored, ids, part, near, flow, 0, half, half * flow.first, False))
    totals = lax.optimization_barrier(totals)
    for stage in range(1, bits):
        for flow, total, got in zip(flows, totals, arrived):
            got.append(cross(send_part(total, got, flow, chips >> (stage + 1)), flow.order[stage]))
    return last_part(count, meta, totals, arrived, flows)


def on_device(stored, tokens, owner_map, live_count):
    count = tokens.shape[0] * lax.axis_size("tensor")
    meta = jnp.stack([lax.axis_index("tensor"), lax.axis_index("sub"), live_count[0]]).astype(jnp.int32)
    step = max(TILE, count // 8)
    heights = list(range(count + TILE, count // 2 + TILE - 1, -step))[::-1]
    which = jnp.clip((live_count[0] + step - heights[0]) // step, 0, len(heights) - 1)
    return lax.switch(which, [functools.partial(run, h) for h in heights], stored, tokens, owner_map, meta)


def solution(mesh):
    placed = (P(("tensor", "sub"), None), P(("groups", "tensor"), None), P(), P("groups"))
    return jax.shard_map(
        on_device,
        mesh=mesh,
        in_specs=placed,
        out_specs=P("groups", ("tensor", "sub")),
        check_vma=False,
    )
```

```python
import functools

import jax
import jax.numpy as jnp
from jax import lax
from jax.experimental import pallas as pl
from jax.experimental.pallas import tpu as pltpu
from jax.sharding import PartitionSpec as P

ORDERS = (
    (2, 0, 1, 3),
    (2, 0, 1, 3),
    (0, 1, 2, 3),
    (1, 2, 3, 0),
)
TURNS = (1,2,3,0)
STEPS = 128.0
TOP = 32000.0
LANES = 256
TILE = 16
VG = 48 * 1024 * 1024
VM = 16 * 1024 * 1024
VP = 16 * 1024 * 1024
VS = 16 * 1024 * 1024
VL = 16 * 1024 * 1024
GROUP = 2
WAIT = 96 * 1024 * 1024


def flow_orders(bits):
    return [[b for b in order if b < bits] + list(range(len(order), bits)) for order in ORDERS]


def flow_blocks(per_dev, flows):
    flows = min(flows, per_dev)
    counts = [per_dev // flows + (1 if f < per_dev % flows else 0) for f in range(flows)]
    firsts = [sum(counts[:f]) for f in range(flows)]
    return list(zip(firsts, counts))


class Flow:
    def __init__(self, order, first, count, per_dev, width, chips):
        self.order, self.first, self.count = order, first, count
        self.per_dev, self.width, self.chips = per_dev, width, chips
        self.bits = len(order)
        self.cols = count * width

    def destination(self, place):
        return sum(((place >> (self.bits - 1 - s)) & 1) << bit for s, bit in enumerate(self.order))

    def spot(self, low):
        return self.first * self.chips + low * self.count


def block_lists(owner, flows):
    chip, sub = lax.axis_index("tensor"), lax.axis_index("sub")
    change = [flow.destination(p) for flow in flows for p in range(flow.chips) for _ in range(flow.count)]
    block = [flow.first + j for flow in flows for _ in range(flow.chips) for j in range(flow.count)]
    per_dev = flows[0].per_dev
    places = [((chip ^ jnp.array(change, jnp.int32)) * 2 + core) * per_dev + jnp.array(block, jnp.int32)
              for core in (sub, 1 - sub)]
    wanted = jnp.concatenate(places)[:, None]
    have = lax.broadcasted_iota(jnp.int32, (1, owner.shape[0]), 1)
    return jnp.sum(jnp.where(wanted == have, owner[None, :], 0), axis=1)


def lanes(index, width):
    return pl.ds(pl.multiple_of(index * width, width), width)


def gather_kernel(runs, width, ids, stored, out, held, sems, out_sems):
    def copy(at, block):
        return pltpu.make_async_copy(stored.at[:, lanes(block, width)], held.at[:, lanes(at, width)], sems.at[at])

    at = 0
    for first, size in runs:
        pl.loop(0, size)(lambda i, at=at, first=first: copy(at + i, ids[first + i]).start())
        at += size
    parts = out_sems.shape[0]
    size = at // parts

    def out_copy(j):
        cols = lanes(j, size * width)
        return pltpu.make_async_copy(held.at[:, cols], out.at[:, cols], out_sems.at[j])

    @pl.loop(0, parts)
    def _(j):
        pl.loop(0, size)(lambda i: copy(j * size + i, 0).wait())
        out_copy(j).start()

    pl.loop(0, parts)(lambda j: out_copy(j).wait())


def gather_for_sibling(stored, ids, flows, low, count):
    rows = stored.shape[0]
    width = flows[0].width
    runs = [(ids.shape[0] // 2 + flow.spot(low), count * flow.count) for flow in flows]
    blocks = sum(size for _, size in runs)
    return pl.pallas_call(
        functools.partial(gather_kernel, runs, width),
        in_specs=[pl.BlockSpec(memory_space=pltpu.SMEM), pl.BlockSpec(memory_space=pltpu.HBM)],
        out_specs=pl.BlockSpec(memory_space=pltpu.HBM),
        out_shape=jax.ShapeDtypeStruct((rows, blocks * width), stored.dtype),
        scratch_shapes=[
            pltpu.VMEM((rows, blocks * width), stored.dtype),
            pltpu.SemaphoreType.DMA((blocks,)),
            pltpu.SemaphoreType.DMA((count,)),
        ],
        compiler_params=pltpu.CompilerParams(vmem_limit_bytes=VG),
        cost_estimate=pl.CostEstimate(flops=0, bytes_accessed=rows, transcendentals=0),
    )(ids, stored)


def decode_scale(code):
    return jnp.exp2(code * (1.0 / STEPS)) * (1.0 / TOP)


def mask_kernel(meta, tok, out):
    rows = tok.shape[1] // 2
    size = min(out.shape[0], tok.shape[0])
    ids = lax.broadcasted_iota(jnp.int32, (size, rows), 0)
    for side in range(2):
        part = tok[:size, lanes(meta[1] ^ side, rows)]
        out[:size, side * rows:(side + 1) * rows] = jnp.where(ids < meta[2], part, jnp.zeros((), tok.dtype))
    if size < out.shape[0]:
        out[size:] = jnp.zeros((out.shape[0] - size, out.shape[1]), out.dtype)


def mask_tokens(height, meta, tokens):
    shape = (height, tokens.shape[1])
    return pl.pallas_call(
        mask_kernel,
        in_specs=[pl.BlockSpec(memory_space=pltpu.SMEM), pl.BlockSpec(memory_space=pltpu.VMEM)],
        out_specs=pl.BlockSpec(memory_space=pltpu.VMEM),
        out_shape=jax.ShapeDtypeStruct(shape, tokens.dtype),
        compiler_params=pltpu.CompilerParams(vmem_limit_bytes=VM),
        cost_estimate=pl.CostEstimate(flops=0, bytes_accessed=WAIT, transcendentals=0),
    )(meta, tokens)


def encode_loop(running, out):
    height = out.shape[0]
    main = height - TILE

    @pl.loop(0, out.shape[1] // LANES)
    def _(c):
        cols = lanes(c, LANES)
        total = running(cols)
        body, tail = total[:main], total[main:]
        is_code = lax.broadcasted_iota(jnp.int32, tail.shape, 0) == TILE - 1
        tail = jnp.where(is_code, 0.0, tail)
        top = jnp.max(jnp.abs(jnp.concatenate([body, tail], axis=0)), axis=0, keepdims=True)
        code = jnp.ceil(jnp.log2(jnp.maximum(top, 1e-30)) * STEPS)
        up = 1.0 / decode_scale(code)
        out[:main, cols] = jnp.round(body * up).astype(jnp.int32).astype(jnp.int16)
        out[main:, cols] = jnp.where(is_code, code, jnp.round(tail * up)).astype(jnp.int32).astype(jnp.int16)


def add_arrived(total, arrived, cols):
    height = total.shape[0]
    for part in arrived:
        code = part[height - TILE:, cols].astype(jnp.float32)[TILE - 1:, :]
        total = total + part[:, cols].astype(jnp.float32) * decode_scale(code)
    return total


def product_kernel(n, coded, ids, tok, *refs):
    out = refs[n + 1]
    own = jnp.concatenate([refs[k][...] for k in range(n)], axis=1)
    weights = jnp.concatenate([own, refs[n][...]], axis=0)
    total = jnp.dot(tok[...], weights, preferred_element_type=jnp.float32)
    if coded:
        held = refs[n + 2]
        held[...] = total
        encode_loop(lambda cols: held[:, cols], out)
    else:
        out[...] = total


def products(stored, ids, tokens, sibling, flow, low, count, sib_first, coded):
    rows = stored.shape[0]
    height = tokens.shape[0]
    group = min(count, GROUP)
    n = group * flow.count
    cols = group * flow.cols

    def pick(k, i, ids):
        return 0, ids[flow.spot(low) + i * n + k]

    kind = jnp.int16 if coded else jnp.float32
    return pl.pallas_call(
        functools.partial(product_kernel, n, coded),
        grid_spec=pltpu.PrefetchScalarGridSpec(
            num_scalar_prefetch=1,
            grid=(count // group,),
            in_specs=[
                pl.BlockSpec(tokens.shape, lambda i, ids: (0, 0)),
                *[pl.BlockSpec((rows, flow.width), functools.partial(pick, k)) for k in range(n)],
                pl.BlockSpec((rows, cols), lambda i, ids: (0, sib_first * flow.width // cols + i)),
            ],
            out_specs=pl.BlockSpec((height, cols), lambda i, ids: (0, i)),
            scratch_shapes=[pltpu.VMEM((height, cols), jnp.float32)] if coded else [],
        ),
        out_shape=jax.ShapeDtypeStruct((height, count * flow.cols), kind),
        compiler_params=pltpu.CompilerParams(vmem_limit_bytes=VP),
        cost_estimate=pl.CostEstimate(
            flops=4 * height * rows * count * flow.cols,
            bytes_accessed=(4 * rows + 4 * height) * count * flow.cols,
            transcendentals=0,
        ),
    )(ids, tokens, *[stored] * n, sibling)


def send_kernel(total, *refs):
    arrived, _, out = refs[:-2], refs[-2], refs[-1]
    encode_loop(lambda cols: add_arrived(total[:, cols], arrived, cols), out)


def send_part(total, arrived, flow, places, after):
    height = total.shape[0]
    group = max(1, places // 2)
    steps = places // group
    block = pl.BlockSpec((height, group * flow.cols), lambda i: (0, steps + i))
    return pl.pallas_call(
        send_kernel,
        grid=(steps,),
        in_specs=[block] * (1 + len(arrived)) + [pl.BlockSpec(memory_space=pl.ANY)],
        out_specs=pl.BlockSpec((height, group * flow.cols), lambda i: (0, i)),
        out_shape=jax.ShapeDtypeStruct((height, places * flow.cols), jnp.int16),
        compiler_params=pltpu.CompilerParams(vmem_limit_bytes=VS),
        cost_estimate=pl.CostEstimate(
            flops=4 * height * places * flow.cols,
            bytes_accessed=(6 + 2 * len(arrived)) * height * places * flow.cols,
            transcendentals=0,
        ),
    )(total, *arrived, after)


def last_kernel(flows, meta, *refs):
    out = refs[-1]
    each = 1 + flows[0].bits
    height = refs[0].shape[0]
    size = min(height, out.shape[0])
    scales = [
        [decode_scale(part[height - TILE:, :].astype(jnp.float32)[TILE - 1:, :])
         for part in refs[f * each + 1:(f + 1) * each]]
        for f in range(len(flows))
    ]

    @pl.loop(0, size // TILE)
    def _(r):
        at = pl.ds(pl.multiple_of(r * TILE, TILE), TILE)
        for f, flow in enumerate(flows):
            x = refs[f * each][at, :]
            for part, scale in zip(refs[f * each + 1:(f + 1) * each], scales[f]):
                x = x + part[at, :].astype(jnp.float32) * scale
            ids = r * TILE + lax.broadcasted_iota(jnp.int32, x.shape, 0)
            cols = pl.ds(flow.first * flow.width, flow.cols)
            out[at, cols] = jnp.where(ids < meta[2], x, 0.0).astype(out.dtype)

    if size < out.shape[0]:
        out[size:] = jnp.zeros((out.shape[0] - size, out.shape[1]), out.dtype)


def last_part(count, meta, totals, arrived, flows):
    height = totals[0].shape[0]
    specs, operands = [], []
    for flow, total, got in zip(flows, totals, arrived):
        specs += [pl.BlockSpec((height, flow.cols), lambda i, meta: (0, 0))] * (1 + len(got))
        operands += [total, *got]
    cols = sum(flow.cols for flow in flows)
    return pl.pallas_call(
        functools.partial(last_kernel, flows),
        grid_spec=pltpu.PrefetchScalarGridSpec(
            num_scalar_prefetch=1,
            grid=(1,),
            in_specs=specs,
            out_specs=pl.BlockSpec((count, cols), lambda i, meta: (0, 0)),
        ),
        out_shape=jax.ShapeDtypeStruct((count, cols), jnp.bfloat16),
        compiler_params=pltpu.CompilerParams(vmem_limit_bytes=VL),
    )(meta, *operands)


def run(height, stored, tokens, owner_map, meta):
    block_count = owner_map.shape[0]
    width = stored.shape[1] // block_count
    chips = lax.axis_size("tensor")
    per_dev = block_count // (2 * chips)
    count = tokens.shape[0] * chips
    bits = chips.bit_length() - 1
    orders = flow_orders(bits)
    flows = [
        Flow(order, first, blocks, per_dev, width, chips)
        for order, (first, blocks) in zip(orders, flow_blocks(per_dev, len(orders)))
    ]

    part = lax.all_to_all(tokens, "tensor", split_axis=1, concat_axis=0, tiled=True)
    half = chips // 2
    ids = block_lists(owner_map, flows)
    swap = lambda x: lax.ppermute(x, "sub", [(0, 1), (1, 0)])
    gather = functools.partial(gather_for_sibling, stored)
    lead = min(1, len(flows) - 1)
    others = [f for f in range(len(flows)) if f != lead]
    first, later = lax.optimization_barrier((swap(gather(ids, [flows[lead]], half, half)), ids))
    far = {lead: (first, 0)}
    if others:
        rest = gather(later, [flows[f] for f in others], half, half)
        rest, later = lax.optimization_barrier((rest, later))
        rest = swap(rest)
        at = 0
        for f in others:
            far[f] = (rest, at)
            at += half * flows[f].count
    picked, part = lax.optimization_barrier((gather(later, flows, 0, half), part))
    near = swap(picked)
    part = mask_tokens(height, meta, part)

    def cross(x, bit):
        return lax.ppermute(x, "tensor", [(c, c ^ (1 << bit)) for c in range(chips)])

    arrived, totals = [], []
    for f, flow in enumerate(flows):
        sibling, at = far[f]
        sent = products(stored, ids, part, sibling, flow, half, half, at, True)
        arrived.append([cross(sent, flow.order[0])])
    for flow in flows:
        totals.append(products(stored, ids, part, near, flow, 0, half, half * flow.first, False))
    totals = lax.optimization_barrier(totals)
    turns = [f for f in TURNS if f < len(flows)]
    after = meta
    for stage in range(1, bits):
        for f in turns:
            after = send_part(totals[f], arrived[f], flows[f], chips >> (stage + 1), after)
            arrived[f].append(cross(after, flows[f].order[stage]))
    return last_part(count, meta, totals, arrived, flows)


def on_device(stored, tokens, owner_map, live_count):
    count = tokens.shape[0] * lax.axis_size("tensor")
    meta = jnp.stack([lax.axis_index("tensor"), lax.axis_index("sub"), live_count[0]]).astype(jnp.int32)
    step = max(TILE, count // 8)
    heights = list(range(count + TILE, count // 2 + TILE - 1, -step))[::-1]
    which = jnp.clip((live_count[0] + step - heights[0]) // step, 0, len(heights) - 1)
    return lax.switch(which, [functools.partial(run, h) for h in heights], stored, tokens, owner_map, meta)


def solution(mesh):
    placed = (P(("tensor", "sub"), None), P(("groups", "tensor"), None), P(), P("groups"))
    return jax.shard_map(
        on_device,
        mesh=mesh,
        in_specs=placed,
        out_specs=P("groups", ("tensor", "sub")),
        check_vma=False,
    )
```
